32 devices in a mesh: term: 4 (over z), sector: 8 (over y, x, core).
Axes of the slice: x: 2, y: 2, z: 4, core: 2. Of those that a mesh axis runs over, the one named last changes fastest.
Arguments:
- left_ops: float32 [4, 8, 512, 512], P('term', 'sector'), may hold values from -1 to 2, as said below
- right_ops: float32 [4, 8, 512, 512], P('term', 'sector'), may hold values from -1 to 2, as said below
- hop_left: float32 [4, 8, 512, 512], P('term', 'sector'), may hold values from -0.09375 to 0.09375
- hop_right: float32 [4, 8, 512, 512], P('term', 'sector'), may hold values from -0.09375 to 0.09375
- v_left: bfloat16 [4, 8, 512, 128], P('term', 'sector'), may hold values from -0.5 to 0.5
- v_right: bfloat16 [4, 8, 128, 512], P('term', 'sector'), may hold values from -1.5 to 1.5
- zero_blocks: bfloat16 [8, 128, 128], P('sector'), may hold values from -6 to 6
- links: int32 [4, 8], P('term', 'sector'), may hold values from 0 to 7
- block_dims: int32 [8], P('sector'), may hold values from 128 to 512
Outputs:
- solution: float32 [8, 512, 512], P('sector')
- residual: float32 [8, 512, 512], P('sector')
The draws below stay inside these ranges and needn't reach their ends.
Inputs may be any that keep to these rules, and one draw needn't show every extreme that they name: Every block left_ops[t, s] and right_ops[t, s] is symmetric and positive definite. `right_ops`: every block is symmetric and positive definite.
All inputs are finite; a program needn't handle non-finite values.
Results may differ from the reference program's by a relative error of at most 0.0003.
Values may be sent and summed in bfloat16 or wider, within the bound.
A program may use at most 64 MiB of HBM per device.

```python
import jax
import jax.numpy as jnp
from jax import lax

BLOCK = 512
ZBLOCK = 128
ITERS = 3
TERMS = 4
SECTORS = 8


def spd_blocks(key, salt):
    key = jax.random.fold_in(key, salt)
    key_noise, key_diag = jax.random.split(key)
    shape = (TERMS, SECTORS, BLOCK, BLOCK)
    noise = jax.random.normal(key_noise, shape, jnp.float32) * (0.12 / BLOCK ** 0.5)
    diag_vals = jnp.exp(jax.random.uniform(key_diag, shape[:3], jnp.float32, jnp.log(0.35), jnp.log(1.2)))
    noise = (noise + jnp.swapaxes(noise, -1, -2)) * 0.7071
    identity = jnp.eye(BLOCK, dtype=jnp.float32)
    return noise + diag_vals[..., None] * identity


def draw_left_ops(key, part):
    return spd_blocks(key, 11)


def draw_right_ops(key, part):
    return spd_blocks(key, 23)


def with_ends(entries, rng, smallest, high):
    longest = entries.shape.index(max(entries.shape))
    spots = []
    for shift in (0, 1):
        where = [jax.random.randint(jax.random.fold_in(rng, axis), (), 0, length) for axis, length in enumerate(entries.shape)]
        where[longest] = (where[longest] + shift) % entries.shape[longest]
        spots.append(tuple(where))
    return entries.at[spots[0]].set(smallest).at[spots[1]].set(high)


def block_scale(key, shape, shards, smallest, largest):
    factor_of, own = 1.0, jax.random.fold_in(key, 6)
    for axis_at, blocks in shards:
        draws = jnp.exp(jax.random.uniform(jax.random.fold_in(own, axis_at), (blocks,), jnp.float32, smallest / len(shards), largest / len(shards)))
        factor_of = factor_of * jnp.repeat(draws, shape[axis_at] // blocks).reshape([-1 if axis == axis_at else 1 for axis in range(len(shape))])
    return factor_of


def bell_draw(own_key, extent, spread, bound, shards=(), held_as=jnp.bfloat16):
    values = jax.random.normal(own_key, extent, jnp.float32) * spread
    if len(shards) > 0:
        values = block_scale(own_key, extent, shards, -0.22, 0.18) * values
    return jnp.clip(values, min=-bound, max=bound).astype(held_as)


def setup_inputs(seed: int = 0) -> dict:
    arg_keys = jax.random.split(jax.random.key(seed), 10)
    left_ops = draw_left_ops(jax.random.fold_in(arg_keys[9], 71), 0)
    right_ops = draw_right_ops(jax.random.fold_in(arg_keys[9], 71), 0)
    hop_left = bell_draw(arg_keys[2], (TERMS, SECTORS, BLOCK, BLOCK), (2 * BLOCK * TERMS) ** -0.5, 0.09375, ((0, 4), (1, 8)), jnp.float32)
    hop_right = bell_draw(arg_keys[3], (TERMS, SECTORS, BLOCK, BLOCK), (2 * BLOCK * TERMS) ** -0.5, 0.09375, ((0, 4), (1, 8)), jnp.float32)
    v_left = bell_draw(arg_keys[4], (TERMS, SECTORS, BLOCK, ZBLOCK), ZBLOCK ** -0.5, 0.5, ((0, 4), (1, 8)))
    v_right = bell_draw(arg_keys[5], (TERMS, SECTORS, ZBLOCK, BLOCK), 0.25, 1.5, ((0, 4), (1, 8)))
    zero_blocks = bell_draw(arg_keys[6], (SECTORS, ZBLOCK, ZBLOCK), 1.0, 6.0, ((0, 8),))
    links = with_ends(jax.random.randint(arg_keys[7], (TERMS, SECTORS), 0, SECTORS), jax.random.fold_in(arg_keys[7], 1), 0, SECTORS - 1).astype(jnp.int32)
    block_dims = with_ends(jax.random.randint(arg_keys[8], (SECTORS,), BLOCK // 4, BLOCK + 1), jax.random.fold_in(arg_keys[8], 1), BLOCK // 4, BLOCK).astype(jnp.int32)
    return dict(left_ops=left_ops, right_ops=right_ops, hop_left=hop_left, hop_right=hop_right, v_left=v_left, v_right=v_right, zero_blocks=zero_blocks, links=links, block_dims=block_dims)


level_gap = 2.5
exact = lax.Precision.HIGHEST


def build_mask(block_dims):
    positions = jnp.arange(BLOCK, dtype=jnp.int32)
    live = positions[None, :] < block_dims[:, None]
    return jnp.logical_and(live[:, :, None], live[:, None, :]).astype(jnp.float32)


def operate(vector, live_mask, left_ops, right_ops, hop_left, hop_right):
    blank = jnp.zeros_like(vector[:1])
    after = jnp.concatenate([vector[1:], blank], 0)
    before = jnp.concatenate([blank, vector[:-1]], 0)

    def one_term(running, operands):
        left_op, right_op, hop_in, hop_out = operands
        inner_part = jnp.einsum('sij,sjk->sik', left_op, vector, precision=exact)
        running = running + jnp.einsum('sik,skl->sil', inner_part, right_op, precision=exact)
        ahead = jnp.einsum('sij,sjk->sik', hop_in, after, precision=exact)
        running = running + jnp.einsum('sik,skl->sil', ahead, hop_out, precision=exact)
        hop_in_prev = jnp.concatenate([jnp.zeros_like(hop_in[:1]), hop_in[:-1]], 0)
        hop_out_prev = jnp.concatenate([jnp.zeros_like(hop_out[:1]), hop_out[:-1]], 0)
        behind = jnp.einsum('sji,sjk->sik', hop_in_prev, before, precision=exact)
        running = running + jnp.einsum('sik,slk->sil', behind, hop_out_prev, precision=exact)
        return running, None

    running, unused = lax.scan(one_term, jnp.zeros(vector.shape, jnp.float32),
                               (left_ops, right_ops, hop_left, hop_right))
    return live_mask * (level_gap * vector + running)


def reference(left_ops, right_ops, hop_left, hop_right, v_left, v_right, zero_blocks, links, block_dims):
    live_mask = build_mask(block_dims)
    picked = zero_blocks[links].astype(jnp.float32)
    middle = jnp.einsum('tsij,tsjk->tsik', v_left.astype(jnp.float32), picked, precision=exact)
    source = -live_mask * jnp.einsum('tsik,tskl->sil', middle, v_right.astype(jnp.float32), precision=exact)
    solution = jnp.zeros_like(source)
    residual = source
    direction = source
    norm_now = jnp.sum(residual * residual)
    for sweep_index in range(ITERS):
        image_vec = operate(direction, live_mask, left_ops, right_ops, hop_left, hop_right)
        step_size = norm_now / jnp.sum(direction * image_vec)
        solution = solution + step_size * direction
        residual = residual - step_size * image_vec
        norm_next = jnp.sum(residual * residual)
        direction = residual + (norm_next / norm_now) * direction
        norm_now = norm_next
    return solution, residual
```

```python
import functools

import jax
import jax.numpy as jnp
from jax import lax
from jax.experimental import pallas as pl
from jax.experimental.pallas import tpu as pltpu
from jax.sharding import PartitionSpec as P

ITERS = 3
CHUNKS = 8
GROUPS = 4

level_gap = 2.5
MESH = pl.DeviceIdType.MESH
f32 = jnp.float32
bf16 = jnp.bfloat16


def halves(value):
    high = value.astype(bf16)
    return high, (value - high.astype(f32)).astype(bf16)


def dot(a, b):
    return jnp.dot(a, b, preferred_element_type=f32)


def dot3(a_high, a_low, b_high, b_low):
    return dot(a_high, b_high) + (dot(a_high, b_low) + dot(a_low, b_high))


def kernel(
    nz, ns, links_ref, dims_ref, left_ref, right_ref, hop_in_ref, hop_out_ref,
    v_left_ref, v_right_ref, zero_ref,
    solution_ref, residual_ref,
    zeros_all, behind_in, behind_out, stage_in, stage_out,
    field_high, field_low, fields, alongs, direction,
    images, part, from_out, from_in, marks_out, marks_in,
    zero_send, zero_recv, hop_send, hop_recv, in_send, in_recv, in_recv2, out_send,
    side_send, side_recv, mark_send, mark_recv,
):
    z = lax.axis_index("term")
    s = lax.axis_index("sector")
    width = fields.shape[-1]
    chunk = width // CHUNKS
    group = width // GROUPS
    per_group = CHUNKS // GROUPS
    mid = nz // 2
    low_half = z < mid
    inward = jnp.where(low_half, z + 1, z - 1)
    outward = jnp.where(low_half, jnp.maximum(z - 1, 0), jnp.minimum(z + 1, nz - 1))
    dist = jnp.where(low_half, mid - 1 - z, z - mid)
    is_mid = dist == 0
    has_out = dist < mid - 1
    has_prev = s > 0
    has_next = s < ns - 1
    before = jnp.maximum(s - 1, 0)
    after = jnp.minimum(s + 1, ns - 1)

    def chunk_rows(c):
        return pl.ds(pl.multiple_of(c * chunk, chunk), chunk)

    def group_rows(g):
        return pl.ds(pl.multiple_of(g * group, group), group)

    barrier = pltpu.get_barrier_semaphore()
    for step in range(1, ns):
        pl.semaphore_signal(
            barrier, inc=1, device_id=(z, lax.rem(s + step, ns)), device_id_type=MESH
        )
    pl.semaphore_signal(barrier, inc=1, device_id=(inward, s), device_id_type=MESH)

    @pl.when(has_out)
    def _():
        pl.semaphore_signal(barrier, inc=1, device_id=(outward, s), device_id_type=MESH)

    pl.semaphore_wait(barrier, ns + jnp.where(has_out, 1, 0))

    def zero_copy(step):
        return pltpu.make_async_remote_copy(
            src_ref=zero_ref,
            dst_ref=zeros_all.at[s],
            send_sem=zero_send.at[step],
            recv_sem=zero_recv.at[step],
            device_id=(z, lax.rem(s + step, ns)),
            device_id_type=MESH,
        )

    for step in range(1, ns):
        zero_copy(step).start()
    zeros_all[s] = zero_ref[...]

    hop_copies = [
        pltpu.make_async_remote_copy(
            src_ref=src,
            dst_ref=dst,
            send_sem=hop_send.at[i],
            recv_sem=hop_recv.at[i],
            device_id=(z, after),
            device_id_type=MESH,
        )
        for i, (src, dst) in enumerate(((hop_in_ref, behind_in), (hop_out_ref, behind_out)))
    ]

    @pl.when(has_next)
    def _():
        for copy in hop_copies:
            copy.start()

    @pl.when(jnp.logical_not(has_prev))
    def _():
        behind_in[...] = jnp.zeros_like(behind_in)
        behind_out[...] = jnp.zeros_like(behind_out)
        for parity in range(2):
            images[parity, 2] = jnp.zeros((width, width), f32)

    @pl.when(jnp.logical_not(has_next))
    def _():
        for parity in range(2):
            images[parity, 1] = jnp.zeros((width, width), f32)

    live_count = dims_ref[0]

    def mask_rows(start, rows):
        row = lax.broadcasted_iota(jnp.int32, (rows, width), 0) + start
        column = lax.broadcasted_iota(jnp.int32, (rows, width), 1)
        live = jnp.logical_and(row < live_count, column < live_count)
        return jnp.where(live, 1.0, 0.0).astype(f32)

    def to_middle(parity, c):
        return pltpu.make_async_remote_copy(
            src_ref=part.at[parity, chunk_rows(c)],
            dst_ref=from_in.at[parity, chunk_rows(c)],
            send_sem=in_send.at[parity, c],
            recv_sem=in_recv.at[parity, c],
            device_id=(inward, s),
            device_id_type=MESH,
        )

    def to_inward(parity, c):
        return pltpu.make_async_remote_copy(
            src_ref=part.at[parity, chunk_rows(c)],
            dst_ref=from_out.at[parity, chunk_rows(c)],
            send_sem=in_send.at[parity, c],
            recv_sem=in_recv2.at[parity, c],
            device_id=(inward, s),
            device_id_type=MESH,
        )

    def to_outward(parity, c):
        return pltpu.make_async_remote_copy(
            src_ref=from_in.at[parity, chunk_rows(c)],
            dst_ref=from_in.at[parity, chunk_rows(c)],
            send_sem=out_send.at[parity, c],
            recv_sem=in_recv.at[parity, c],
            device_id=(outward, s),
            device_id_type=MESH,
        )

    def to_side(parity, c, which):
        return pltpu.make_async_remote_copy(
            src_ref=images.at[parity, 0, chunk_rows(c)],
            dst_ref=images.at[parity, which, chunk_rows(c)],
            send_sem=side_send.at[parity, which - 1, c],
            recv_sem=side_recv.at[parity, which - 1, c],
            device_id=(z, before if which == 1 else after),
            device_id_type=MESH,
        )

    def reduce_rows(parity, produce, finish, share):
        most = 2 + 2 * (mid - 1)
        lag = 2 + 2 * dist

        def one(c, carry):
            @pl.when(c < CHUNKS)
            def _():
                @pl.when(lax.rem(c, per_group) == 0)
                def _():
                    produce(c // per_group)

                @pl.when(has_out)
                def _():
                    to_inward(parity, c).wait_recv()
                    part[parity, chunk_rows(c)] = (
                        part[parity, chunk_rows(c)] + from_out[parity, chunk_rows(c)]
                    )

                @pl.when(is_mid)
                def _():
                    to_middle(parity, c).start()

                @pl.when(jnp.logical_not(is_mid))
                def _():
                    to_inward(parity, c).start()

            @pl.when(jnp.logical_and(c >= lag, c < CHUNKS + lag))
            def _():
                d = c - lag
                to_middle(parity, d).wait_recv()

                @pl.when(is_mid)
                def _():
                    from_in[parity, chunk_rows(d)] = (
                        part[parity, chunk_rows(d)] + from_in[parity, chunk_rows(d)]
                    )

                @pl.when(has_out)
                def _():
                    to_outward(parity, d).start()

                images[parity, 0, chunk_rows(d)] = finish(from_in[parity, chunk_rows(d)], d)

                if share:
                    @pl.when(has_prev)
                    def _():
                        to_side(parity, d, 1).start()

                    @pl.when(has_next)
                    def _():
                        to_side(parity, d, 2).start()

            return carry

        lax.fori_loop(0, CHUNKS + most, one, 0)

    def settle(parity, share):
        def one(c, carry):
            to_middle(parity, c).wait_send()

            @pl.when(has_out)
            def _():
                to_outward(parity, c).wait_send()

            if share:
                @pl.when(has_prev)
                def _():
                    to_side(parity, c, 1).wait_send()
                    to_side(parity, c, 2).wait_recv()

                @pl.when(has_next)
                def _():
                    to_side(parity, c, 2).wait_send()
                    to_side(parity, c, 1).wait_recv()

            return carry

        lax.fori_loop(0, CHUNKS, one, 0)

    for step in range(1, ns):
        zero_copy(step).wait()
    picked = zeros_all[links_ref[0, 0]]

    def source_rows(g):
        rows = group_rows(g)
        middle = dot(v_left_ref[rows, :], picked)
        high, rest = halves(middle)
        low = (middle - high.astype(f32)) - rest.astype(f32)
        v_right = v_right_ref[...]
        part[0, rows] = dot(high, v_right) + (
            dot(rest, v_right) + dot(low.astype(bf16), v_right)
        )

    def source_end(total, c):
        return -mask_rows(c * chunk, chunk) * total

    def split_into(slot, target, value, rows):
        high, low = halves(value)
        target[slot, 0, rows] = high
        target[slot, 1, rows] = low

    for g in range(GROUPS):
        rows = slice(g * group, (g + 1) * group)
        split_into(0, stage_in, left_ref[rows, :], rows)
        split_into(1, stage_in, hop_in_ref[rows, :], rows)
        split_into(0, stage_out, right_ref[rows, :], rows)
        split_into(1, stage_out, hop_out_ref[rows, :], rows)

    reduce_rows(0, source_rows, source_end, True)

    @pl.when(has_prev)
    def _():
        for copy in hop_copies:
            copy.wait_recv()

    for g in range(GROUPS):
        rows = slice(g * group, (g + 1) * group)
        split_into(2, stage_in, behind_in[:, rows].T, rows)
        split_into(2, stage_out, behind_out[:, rows].T, rows)

    settle(0, True)

    def fold(value):
        rows = value.shape[0]
        total = jnp.sum(value.reshape(rows // 8, 8, width), axis=0)
        return sum(total[:, i:i + 128] for i in range(0, width, 128))

    def begin(c, carry):
        rows = chunk_rows(c)
        marks = jnp.zeros((8, 128), f32)
        for which in range(3):
            value = images[0, which, rows]
            fields[which, rows] = value
            alongs[which, rows] = jnp.zeros_like(value)
            high, low = halves(value)
            field_high[which, rows] = high
            field_low[which, rows] = low
            if which == 0:
                marks = fold(value * value)
        direction[rows] = jnp.zeros((chunk, width), f32)
        solution_ref[rows, :] = jnp.zeros((chunk, width), f32)
        return carry + marks

    norm_marks = lax.fori_loop(0, CHUNKS, begin, jnp.zeros((8, 128), f32))

    def operator_rows(parity):
        def rows_of(g):
            rows = group_rows(g)
            total = None
            for which in range(3):
                first = dot3(
                    stage_in[which, 0, rows], stage_in[which, 1, rows],
                    field_high[which], field_low[which],
                )
                high, low = halves(first)
                second = dot3(high, low, stage_out[which, 0], stage_out[which, 1])
                total = second if total is None else total + second
            part[parity, rows] = total
        return rows_of

    norm_before = jnp.ones((1, 1), f32)
    step_size = jnp.ones((1, 1), f32)
    for sweep in range(ITERS):
        last = sweep + 1 == ITERS
        parity = (sweep + 1) % 2

        marks_out[sweep, 0:8] = norm_marks
        marks_out[sweep, 8:16] = jnp.zeros((8, 128), f32)

        def image_end(total, c):
            rows = chunk_rows(c)
            own = fields[0, rows]
            image = mask_rows(c * chunk, chunk) * (level_gap * own + total)
            marks_out[sweep, 8:16] = marks_out[sweep, 8:16] + fold(own * image)
            return image

        reduce_rows(parity, operator_rows(parity), image_end, not last)

        def mark_copy(step):
            return pltpu.make_async_remote_copy(
                src_ref=marks_out.at[sweep],
                dst_ref=marks_in.at[sweep, s],
                send_sem=mark_send.at[sweep, step],
                recv_sem=mark_recv.at[sweep, step],
                device_id=(z, lax.rem(s + step, ns)),
                device_id_type=MESH,
            )

        for step in range(1, ns):
            mark_copy(step).start()
        marks_in[sweep, s] = marks_out[sweep]
        settle(parity, not last)
        for step in range(1, ns):
            mark_copy(step).wait()
        summed = jnp.sum(marks_in[sweep], axis=0)
        norm_now = jnp.sum(summed[0:8], keepdims=True)
        product = jnp.sum(summed[8:16], keepdims=True)
        if sweep == 0:
            ratio = jnp.zeros((1, 1), f32)
            step_size = norm_now / product
        else:
            ratio = norm_now / norm_before
            step_size = norm_now / (product - ratio * norm_now / step_size)
        norm_before = norm_now

        def update(c, carry, ratio=ratio, step_size=step_size, parity=parity, last=last):
            rows = chunk_rows(c)
            old = fields[0, rows]
            heading = old + ratio * direction[rows]
            solution_ref[rows, :] = solution_ref[rows, :] + step_size * heading
            if last:
                along = images[parity, 0, rows] + ratio * alongs[0, rows]
                residual_ref[rows, :] = old - step_size * along
                return carry
            direction[rows] = heading
            marks = None
            for which in range(3):
                along = images[parity, which, rows] + ratio * alongs[which, rows]
                value = fields[which, rows] - step_size * along
                alongs[which, rows] = along
                fields[which, rows] = value
                high, low = halves(value)
                field_high[which, rows] = high
                field_low[which, rows] = low
                if which == 0:
                    marks = fold(value * value)
            return carry + marks

        norm_marks = lax.fori_loop(0, CHUNKS, update, jnp.zeros((8, 128), f32))

    @pl.when(has_next)
    def _():
        for copy in hop_copies:
            copy.wait_send()


def body(left_ops, right_ops, hop_left, hop_right, v_left, v_right, zero_blocks, links, block_dims):
    width = left_ops.shape[-1]
    small = zero_blocks.shape[-1]
    nz = lax.axis_size("term")
    ns = lax.axis_size("sector")
    vmem = pl.BlockSpec(memory_space=pltpu.VMEM)
    smem = pl.BlockSpec(memory_space=pltpu.SMEM)
    dma = pltpu.SemaphoreType.DMA
    square = jax.ShapeDtypeStruct((width, width), f32)
    solution, residual = pl.pallas_call(
        functools.partial(kernel, nz, ns),
        out_shape=(square, square),
        in_specs=[smem, smem] + [vmem] * 7,
        out_specs=(vmem, vmem),
        scratch_shapes=[
            pltpu.VMEM((ns, small, small), bf16),
            pltpu.VMEM((width, width), f32),
            pltpu.VMEM((width, width), f32),
            pltpu.VMEM((3, 2, width, width), bf16),
            pltpu.VMEM((3, 2, width, width), bf16),
            pltpu.VMEM((3, width, width), bf16),
            pltpu.VMEM((3, width, width), bf16),
            pltpu.VMEM((3, width, width), f32),
            pltpu.VMEM((3, width, width), f32),
            pltpu.VMEM((width, width), f32),
            pltpu.VMEM((2, 3, width, width), f32),
            pltpu.VMEM((2, width, width), f32),
            pltpu.VMEM((2, width, width), f32),
            pltpu.VMEM((2, width, width), f32),
            pltpu.VMEM((ITERS, 16, 128), f32),
            pltpu.VMEM((ITERS, ns, 16, 128), f32),
            dma((ns,)),
            dma((ns,)),
            dma((2,)),
            dma((2,)),
            dma((2, CHUNKS)),
            dma((2, CHUNKS)),
            dma((2, CHUNKS)),
            dma((2, CHUNKS)),
            dma((2, 2, CHUNKS)),
            dma((2, 2, CHUNKS)),
            dma((ITERS, ns)),
            dma((ITERS, ns)),
        ],
        compiler_params=pltpu.CompilerParams(
            collective_id=0, has_side_effects=True, vmem_limit_bytes=56 * 1024 * 1024
        ),
        cost_estimate=pl.CostEstimate(
            flops=ITERS * 36 * width ** 3, bytes_accessed=24 * width * width, transcendentals=0
        ),
    )(
        links, block_dims, left_ops[0, 0], right_ops[0, 0], hop_left[0, 0], hop_right[0, 0],
        v_left[0, 0], v_right[0, 0], zero_blocks[0],
    )
    return solution[None], residual[None]


def solution(mesh):
    return jax.shard_map(
        body,
        mesh=mesh,
        in_specs=(
            P("term", "sector", None, None),
            P("term", "sector", None, None),
            P("term", "sector", None, None),
            P("term", "sector", None, None),
            P("term", "sector", None, None),
            P("term", "sector", None, None),
            P("sector", None, None),
            P("term", "sector"),
            P("sector"),
        ),
        out_specs=(P("sector", None, None), P("sector", None, None)),
        check_vma=False,
    )
```

```python
import functools

import jax
import jax.numpy as jnp
from jax import lax
from jax.experimental import pallas as pl
from jax.experimental.pallas import tpu as pltpu
from jax.sharding import PartitionSpec as P

ITERS = 3
CHUNKS = 16
GROUPS = 4
LAG = 3
LAG_STEP = 6

level_gap = 2.5
MESH = pl.DeviceIdType.MESH
f32 = jnp.float32
bf16 = jnp.bfloat16


def halves(value):
    high = value.astype(bf16)
    return high, (value - high.astype(f32)).astype(bf16)


def dot(a, b):
    return jnp.dot(a, b, preferred_element_type=f32)


def dot3(a_high, a_low, b_high, b_low):
    return dot(a_high, b_high) + (dot(a_high, b_low) + dot(a_low, b_high))


def kernel(
    nz, ns, links_ref, dims_ref, left_ref, right_ref, hop_in_ref, hop_out_ref,
    v_left_ref, v_right_ref, zero_ref,
    solution_ref, residual_ref,
    zeros_all, behind_in, behind_out, stage_in, stage_out,
    field_high, field_low, fields, alongs, direction,
    images, part, from_out, from_in, marks_out, marks_in,
    zero_send, zero_recv, hop_send, hop_recv, in_send, in_recv, in_recv2, out_send,
    side_send, side_recv, mark_send, mark_recv,
):
    z = lax.axis_index("term")
    s = lax.axis_index("sector")
    width = fields.shape[-1]
    chunk = width // CHUNKS
    group = width // GROUPS
    per_group = CHUNKS // GROUPS
    mid = nz // 2
    low_half = z < mid
    inward = jnp.where(low_half, z + 1, z - 1)
    outward = jnp.where(low_half, jnp.maximum(z - 1, 0), jnp.minimum(z + 1, nz - 1))
    dist = jnp.where(low_half, mid - 1 - z, z - mid)
    is_mid = dist == 0
    has_out = dist < mid - 1
    has_prev = s > 0
    has_next = s < ns - 1
    before = jnp.maximum(s - 1, 0)
    after = jnp.minimum(s + 1, ns - 1)

    def chunk_rows(c):
        return pl.ds(pl.multiple_of(c * chunk, chunk), chunk)

    def group_rows(g):
        return pl.ds(pl.multiple_of(g * group, group), group)

    barrier = pltpu.get_barrier_semaphore()
    for step in range(1, ns):
        pl.semaphore_signal(
            barrier, inc=1, device_id=(z, lax.rem(s + step, ns)), device_id_type=MESH
        )
    pl.semaphore_signal(barrier, inc=1, device_id=(inward, s), device_id_type=MESH)

    @pl.when(has_out)
    def _():
        pl.semaphore_signal(barrier, inc=1, device_id=(outward, s), device_id_type=MESH)

    pl.semaphore_wait(barrier, ns + jnp.where(has_out, 1, 0))

    def zero_copy(step):
        return pltpu.make_async_remote_copy(
            src_ref=zero_ref,
            dst_ref=zeros_all.at[s],
            send_sem=zero_send.at[step],
            recv_sem=zero_recv.at[step],
            device_id=(z, lax.rem(s + step, ns)),
            device_id_type=MESH,
        )

    for step in range(1, ns):
        zero_copy(step).start()
    zeros_all[s] = zero_ref[...]

    hop_copies = [
        pltpu.make_async_remote_copy(
            src_ref=src,
            dst_ref=dst,
            send_sem=hop_send.at[i],
            recv_sem=hop_recv.at[i],
            device_id=(z, after),
            device_id_type=MESH,
        )
        for i, (src, dst) in enumerate(((hop_in_ref, behind_in), (hop_out_ref, behind_out)))
    ]

    @pl.when(has_next)
    def _():
        for copy in hop_copies:
            copy.start()

    @pl.when(jnp.logical_not(has_prev))
    def _():
        behind_in[...] = jnp.zeros_like(behind_in)
        behind_out[...] = jnp.zeros_like(behind_out)
        for parity in range(2):
            images[parity, 2] = jnp.zeros((width, width), f32)

    @pl.when(jnp.logical_not(has_next))
    def _():
        for parity in range(2):
            images[parity, 1] = jnp.zeros((width, width), f32)

    live_count = dims_ref[0]

    def mask_rows(start, rows):
        row = lax.broadcasted_iota(jnp.int32, (rows, width), 0) + start
        column = lax.broadcasted_iota(jnp.int32, (rows, width), 1)
        live = jnp.logical_and(row < live_count, column < live_count)
        return jnp.where(live, 1.0, 0.0).astype(f32)

    def to_middle(parity, c):
        return pltpu.make_async_remote_copy(
            src_ref=part.at[parity, chunk_rows(c)],
            dst_ref=from_in.at[parity, chunk_rows(c)],
            send_sem=in_send.at[parity, c],
            recv_sem=in_recv.at[parity, c],
            device_id=(inward, s),
            device_id_type=MESH,
        )

    def to_inward(parity, c):
        return pltpu.make_async_remote_copy(
            src_ref=part.at[parity, chunk_rows(c)],
            dst_ref=from_out.at[parity, chunk_rows(c)],
            send_sem=in_send.at[parity, c],
            recv_sem=in_recv2.at[parity, c],
            device_id=(inward, s),
            device_id_type=MESH,
        )

    def to_outward(parity, c):
        return pltpu.make_async_remote_copy(
            src_ref=from_in.at[parity, chunk_rows(c)],
            dst_ref=from_in.at[parity, chunk_rows(c)],
            send_sem=out_send.at[parity, c],
            recv_sem=in_recv.at[parity, c],
            device_id=(outward, s),
            device_id_type=MESH,
        )

    def to_side(parity, c, which):
        return pltpu.make_async_remote_copy(
            src_ref=images.at[parity, 0, chunk_rows(c)],
            dst_ref=images.at[parity, which, chunk_rows(c)],
            send_sem=side_send.at[parity, which - 1, c],
            recv_sem=side_recv.at[parity, which - 1, c],
            device_id=(z, before if which == 1 else after),
            device_id_type=MESH,
        )

    def reduce_rows(parity, produce, finish, share):
        most = LAG + LAG_STEP * (mid - 1)
        lag = LAG + LAG_STEP * dist

        def one(c, carry):
            @pl.when(c < CHUNKS)
            def _():
                @pl.when(lax.rem(c, per_group) == 0)
                def _():
                    produce(c // per_group)

                @pl.when(has_out)
                def _():
                    to_inward(parity, c).wait_recv()
                    part[parity, chunk_rows(c)] = (
                        part[parity, chunk_rows(c)] + from_out[parity, chunk_rows(c)]
                    )

                @pl.when(is_mid)
                def _():
                    to_middle(parity, c).start()

                @pl.when(jnp.logical_not(is_mid))
                def _():
                    to_inward(parity, c).start()

            @pl.when(jnp.logical_and(c >= lag, c < CHUNKS + lag))
            def _():
                d = c - lag
                to_middle(parity, d).wait_recv()

                @pl.when(is_mid)
                def _():
                    from_in[parity, chunk_rows(d)] = (
                        part[parity, chunk_rows(d)] + from_in[parity, chunk_rows(d)]
                    )

                @pl.when(has_out)
                def _():
                    to_outward(parity, d).start()

                images[parity, 0, chunk_rows(d)] = finish(from_in[parity, chunk_rows(d)], d)

                if share:
                    @pl.when(has_prev)
                    def _():
                        to_side(parity, d, 1).start()

                    @pl.when(has_next)
                    def _():
                        to_side(parity, d, 2).start()

            return carry

        lax.fori_loop(0, CHUNKS + most, one, 0)

    def settle(parity, share):
        def one(c, carry):
            to_middle(parity, c).wait_send()

            @pl.when(has_out)
            def _():
                to_outward(parity, c).wait_send()

            if share:
                @pl.when(has_prev)
                def _():
                    to_side(parity, c, 1).wait_send()
                    to_side(parity, c, 2).wait_recv()

                @pl.when(has_next)
                def _():
                    to_side(parity, c, 2).wait_send()
                    to_side(parity, c, 1).wait_recv()

            return carry

        lax.fori_loop(0, CHUNKS, one, 0)

    for step in range(1, ns):
        zero_copy(step).wait()
    picked = zeros_all[links_ref[0, 0]]

    def source_rows(g):
        rows = group_rows(g)
        middle = dot(v_left_ref[rows, :], picked)
        high, rest = halves(middle)
        low = (middle - high.astype(f32)) - rest.astype(f32)
        v_right = v_right_ref[...]
        part[0, rows] = dot(high, v_right) + (
            dot(rest, v_right) + dot(low.astype(bf16), v_right)
        )

    def source_end(total, c):
        return -mask_rows(c * chunk, chunk) * total

    def split_into(slot, target, value, rows):
        high, low = halves(value)
        target[slot, 0, rows] = high
        target[slot, 1, rows] = low

    for g in range(GROUPS):
        rows = slice(g * group, (g + 1) * group)
        split_into(0, stage_in, left_ref[rows, :], rows)
        split_into(1, stage_in, hop_in_ref[rows, :], rows)
        split_into(0, stage_out, right_ref[rows, :], rows)
        split_into(1, stage_out, hop_out_ref[rows, :], rows)

    reduce_rows(0, source_rows, source_end, True)

    @pl.when(has_prev)
    def _():
        for copy in hop_copies:
            copy.wait_recv()

    for g in range(GROUPS):
        rows = slice(g * group, (g + 1) * group)
        split_into(2, stage_in, behind_in[:, rows].T, rows)
        split_into(2, stage_out, behind_out[:, rows].T, rows)

    settle(0, True)

    def fold(value):
        rows = value.shape[0]
        total = jnp.sum(value.reshape(rows // 8, 8, width), axis=0)
        return sum(total[:, i:i + 128] for i in range(0, width, 128))

    def begin(c, carry):
        rows = chunk_rows(c)
        marks = jnp.zeros((8, 128), f32)
        for which in range(3):
            value = images[0, which, rows]
            fields[which, rows] = value
            alongs[which, rows] = jnp.zeros_like(value)
            high, low = halves(value)
            field_high[which, rows] = high
            field_low[which, rows] = low
            if which == 0:
                marks = fold(value * value)
        direction[rows] = jnp.zeros((chunk, width), f32)
        solution_ref[rows, :] = jnp.zeros((chunk, width), f32)
        return carry + marks

    norm_marks = lax.fori_loop(0, CHUNKS, begin, jnp.zeros((8, 128), f32))

    def operator_rows(parity):
        def rows_of(g):
            rows = group_rows(g)
            total = None
            for which in range(3):
                first = dot3(
                    stage_in[which, 0, rows], stage_in[which, 1, rows],
                    field_high[which], field_low[which],
                )
                high, low = halves(first)
                second = dot3(high, low, stage_out[which, 0], stage_out[which, 1])
                total = second if total is None else total + second
            part[parity, rows] = total
        return rows_of

    norm_before = jnp.ones((1, 1), f32)
    step_size = jnp.ones((1, 1), f32)
    for sweep in range(ITERS):
        last = sweep + 1 == ITERS
        parity = (sweep + 1) % 2

        marks_out[sweep, 0:8] = norm_marks
        marks_out[sweep, 8:16] = jnp.zeros((8, 128), f32)

        def image_end(total, c):
            rows = chunk_rows(c)
            own = fields[0, rows]
            image = mask_rows(c * chunk, chunk) * (level_gap * own + total)
            marks_out[sweep, 8:16] = marks_out[sweep, 8:16] + fold(own * image)
            return image

        reduce_rows(parity, operator_rows(parity), image_end, not last)

        def mark_copy(step):
            return pltpu.make_async_remote_copy(
                src_ref=marks_out.at[sweep],
                dst_ref=marks_in.at[sweep, s],
                send_sem=mark_send.at[sweep, step],
                recv_sem=mark_recv.at[sweep, step],
                device_id=(z, lax.rem(s + step, ns)),
                device_id_type=MESH,
            )

        for step in range(1, ns):
            mark_copy(step).start()
        marks_in[sweep, s] = marks_out[sweep]
        settle(parity, not last)
        for step in range(1, ns):
            mark_copy(step).wait()
        summed = jnp.sum(marks_in[sweep], axis=0)
        norm_now = jnp.sum(summed[0:8], keepdims=True)
        product = jnp.sum(summed[8:16], keepdims=True)
        if sweep == 0:
            ratio = jnp.zeros((1, 1), f32)
            step_size = norm_now / product
        else:
            ratio = norm_now / norm_before
            step_size = norm_now / (product - ratio * norm_now / step_size)
        norm_before = norm_now

        def update(c, carry, ratio=ratio, step_size=step_size, parity=parity, last=last):
            rows = chunk_rows(c)
            old = fields[0, rows]
            heading = old + ratio * direction[rows]
            solution_ref[rows, :] = solution_ref[rows, :] + step_size * heading
            if last:
                along = images[parity, 0, rows] + ratio * alongs[0, rows]
                residual_ref[rows, :] = old - step_size * along
                return carry
            direction[rows] = heading
            marks = None
            for which in range(3):
                along = images[parity, which, rows] + ratio * alongs[which, rows]
                value = fields[which, rows] - step_size * along
                alongs[which, rows] = along
                fields[which, rows] = value
                high, low = halves(value)
                field_high[which, rows] = high
                field_low[which, rows] = low
                if which == 0:
                    marks = fold(value * value)
            return carry + marks

        norm_marks = lax.fori_loop(0, CHUNKS, update, jnp.zeros((8, 128), f32))

    @pl.when(has_next)
    def _():
        for copy in hop_copies:
            copy.wait_send()


def body(left_ops, right_ops, hop_left, hop_right, v_left, v_right, zero_blocks, links, block_dims):
    width = left_ops.shape[-1]
    small = zero_blocks.shape[-1]
    nz = lax.axis_size("term")
    ns = lax.axis_size("sector")
    vmem = pl.BlockSpec(memory_space=pltpu.VMEM)
    smem = pl.BlockSpec(memory_space=pltpu.SMEM)
    dma = pltpu.SemaphoreType.DMA
    square = jax.ShapeDtypeStruct((width, width), f32)
    solution, residual = pl.pallas_call(
        functools.partial(kernel, nz, ns),
        out_shape=(square, square),
        in_specs=[smem, smem] + [vmem] * 7,
        out_specs=(vmem, vmem),
        scratch_shapes=[
            pltpu.VMEM((ns, small, small), bf16),
            pltpu.VMEM((width, width), f32),
            pltpu.VMEM((width, width), f32),
            pltpu.VMEM((3, 2, width, width), bf16),
            pltpu.VMEM((3, 2, width, width), bf16),
            pltpu.VMEM((3, width, width), bf16),
            pltpu.VMEM((3, width, width), bf16),
            pltpu.VMEM((3, width, width), f32),
            pltpu.VMEM((3, width, width), f32),
            pltpu.VMEM((width, width), f32),
            pltpu.VMEM((2, 3, width, width), f32),
            pltpu.VMEM((2, width, width), f32),
            pltpu.VMEM((2, width, width), f32),
            pltpu.VMEM((2, width, width), f32),
            pltpu.VMEM((ITERS, 16, 128), f32),
            pltpu.VMEM((ITERS, ns, 16, 128), f32),
            dma((ns,)),
            dma((ns,)),
            dma((2,)),
            dma((2,)),
            dma((2, CHUNKS)),
            dma((2, CHUNKS)),
            dma((2, CHUNKS)),
            dma((2, CHUNKS)),
            dma((2, 2, CHUNKS)),
            dma((2, 2, CHUNKS)),
            dma((ITERS, ns)),
            dma((ITERS, ns)),
        ],
        compiler_params=pltpu.CompilerParams(
            collective_id=0, has_side_effects=True, vmem_limit_bytes=56 * 1024 * 1024
        ),
        cost_estimate=pl.CostEstimate(
            flops=ITERS * 36 * width ** 3, bytes_accessed=24 * width * width, transcendentals=0
        ),
    )(
        links, block_dims, left_ops[0, 0], right_ops[0, 0], hop_left[0, 0], hop_right[0, 0],
        v_left[0, 0], v_right[0, 0], zero_blocks[0],
    )
    return solution[None], residual[None]


def solution(mesh):
    return jax.shard_map(
        body,
        mesh=mesh,
        in_specs=(
            P("term", "sector", None, None),
            P("term", "sector", None, None),
            P("term", "sector", None, None),
            P("term", "sector", None, None),
            P("term", "sector", None, None),
            P("term", "sector", None, None),
            P("sector", None, None),
            P("term", "sector"),
            P("sector"),
        ),
        out_specs=(P("sector", None, None), P("sector", None, None)),
        check_vma=False,
    )
```
